32 devices in a mesh: src: 4 (over x, core), frame: 2 (over y), tile: 4 (over z).
Axes of the slice: x: 2, y: 2, z: 4, core: 2. Of those that a mesh axis runs over, the one named last changes fastest.
Arguments:
- feats: float32 [49152, 512], P(('src', 'frame', 'tile')), may hold values from -40 to 40
- row_map: int32 [49152], P(('src', 'frame', 'tile')), may hold values from 0 to 49151, as said below
- clip_ids: int32 [12], replicated, may hold values from 0 to 3, never falling along the last dimension, each value on 1 to 6 neighbouring positions
- norm_gain: float32 [512], replicated, may hold values from 0.1 to 1.9
- norm_bias: float32 [512], replicated, may hold values from -3 to 3
- conv_weight: bfloat16 [3, 3, 3, 512, 512], replicated, may hold values from -0.0546875 to 0.0546875
- conv_bias: float32 [512], replicated, may hold values from -2 to 2
Outputs:
- decoded: bfloat16 [12, 32, 128, 512], P('frame', 'tile', 'src')
The draws below stay inside these ranges and needn't reach their ends.
Inputs may be any that keep to these rules, and one draw needn't show every extreme that they name: `row_map`: every decoder index occurs once; the rows of each device of src+frame+tile hold exactly 48 indices of each aligned block of 1536 decoder indices. `clip_ids`: clip numbers never fall along the frames; each clip has 1 to 6 frames, one exactly 6.
All inputs are finite; a program needn't handle non-finite values.
Results may differ from the reference program's by a relative error of at most 0.0029.
Values may be sent and summed in bfloat16 or wider, within the bound.
A program may use at most 128 MiB of HBM per device.

```python
import math
import jax
import jax.numpy as jnp
import numpy as np
from jax import lax

C = 512
GROUPS = 32
CLIPS = 4
FR_DEV = 6
HR = 8
WCOL = 32
VOX_DEV = 1536
ALL_ROWS = 49152
PER_PAIR = 48
FRAMES = 12
HEIGHT = 32
WIDTH = 128
MOST = 6
N_SRC = 4
N_FRAME = 2
N_TILE = 4


feature_level = 0.1


def shuffled(subkey):
    return jax.random.permutation(subkey, VOX_DEV).astype(jnp.int32)


def row_layout(key):
    devices = ALL_ROWS // VOX_DEV
    source_keys = jax.random.split(jax.random.fold_in(key, 1), devices)
    owner_keys = jax.random.split(jax.random.fold_in(key, 2), devices)
    source_perm = jax.vmap(shuffled)(source_keys)
    owner_perm = jax.vmap(shuffled)(owner_keys)
    owners = source_perm // PER_PAIR
    within = source_perm % PER_PAIR
    senders = jnp.arange(devices, dtype=jnp.int32)[:, None]
    slot_ids = owner_perm[owners, senders * PER_PAIR + within]
    return (owners * VOX_DEV + slot_ids).reshape(-1).astype(jnp.int32)


def draw_row_map(key, part):
    return row_layout(jax.random.fold_in(key, 11))


def draw_feats(key, part):
    targets = row_layout(jax.random.fold_in(key, 11))
    n_frame = FRAMES // FR_DEV
    n_tile = HEIGHT // HR
    device = targets // VOX_DEV
    inner = targets % VOX_DEV
    width_block = device // (n_frame * n_tile)
    frame_block = device // n_tile % n_frame
    tile_block = device % n_tile
    height_index = tile_block * HR + inner // WCOL % HR
    width_index = width_block * WCOL + inner % WCOL
    parity_sign = ((height_index + width_index) % 2 * 2 - 1).astype(jnp.float32)
    frame_pos = (frame_block * FR_DEV + inner // (HR * WCOL)).astype(jnp.float32) / FRAMES
    height_pos = height_index.astype(jnp.float32) / HEIGHT
    width_pos = width_index.astype(jnp.float32) / WIDTH
    noise_rows = jax.random.uniform(jax.random.fold_in(key, 21), (ALL_ROWS,), jnp.float32, 0.0, math.log(3.0))
    row_scale = jnp.exp(width_pos * math.log(3.0) + height_pos * math.log(1.6) + frame_pos * math.log(3.0) + noise_rows)
    col_scale = jnp.exp(jax.random.uniform(jax.random.fold_in(key, 22), (C,), jnp.float32, math.log(0.5), math.log(2.0)))
    group_sign = (jax.random.randint(jax.random.fold_in(key, 31), (GROUPS,), 0, 2) * 2 - 1).astype(jnp.float32)
    channel_sign = jnp.repeat(group_sign, C // GROUPS)
    channel_size = jax.random.uniform(jax.random.fold_in(key, 32), (C,), jnp.float32, 1.0, 2.0)
    channel_offset = 3.0 * channel_sign * channel_size * col_scale
    base = jnp.clip(jax.random.normal(jax.random.fold_in(key, 23), (ALL_ROWS, C), jnp.float32), -4.0, 4.0)
    place_factor = 0.3 + 0.4 * frame_pos + 0.8 * width_pos + 1.2 * width_pos * width_pos + 0.6 * height_pos + 0.1 * parity_sign
    spread_part = base * row_scale[:, None] * col_scale[None, :]
    offset_part = place_factor[:, None] * channel_offset[None, :]
    return (feature_level * (spread_part + offset_part)).astype(jnp.float32)


def split_up(count, total, bound, slope):
    portions = [(1 << 20) // math.isqrt(standing ** slope) + 1 for standing in range(2, count + 1)]
    surplus, holding = total - bound - (count - 1), [1] * (count - 1)
    while surplus > 0:
        candidates = [i for i in range(count - 1) if holding[i] < bound]
        whole, remaining = sum([portions[i] for i in candidates]), surplus
        for i in candidates:
            extra = min(bound - holding[i], max(1, remaining * portions[i] // whole), surplus)
            holding[i] = holding[i] + extra
            surplus = surplus - extra
    return np.array([bound] + holding)


def ragged(stream_key, number_of, total, most, skew):
    if number_of == 2:
        one = jax.random.randint(stream_key, (), max(1, total - most), min(most, total - 1) + 1)
        return jnp.stack([one, total - one])
    lengths = jnp.asarray(split_up(number_of, total, most, skew), jnp.int32)
    twos = (number_of - 1) // 2
    donor, receiver = lengths[1:1 + 2 * twos:2], lengths[2:2 + 2 * twos:2]
    slack = jnp.minimum(donor - 1, most - receiver)
    moved = jax.random.randint(jax.random.fold_in(stream_key, 1), (twos,), 0, 1 << 20) % (slack + 1)
    lengths = lengths.at[1:1 + 2 * twos:2].set(donor - moved).at[2:2 + 2 * twos:2].set(receiver + moved)
    return lengths[jax.random.permutation(jax.random.fold_in(stream_key, 2), number_of)]


def normal_values(rng, dims, deviation, most, held_as=jnp.bfloat16):
    return jnp.clip(deviation * jax.random.normal(rng, dims, jnp.float32), -most, most).astype(held_as)


def setup_inputs(seed: int = 0) -> dict:
    key_of = jax.random.split(jax.random.key(seed), 8)
    return {
        "feats": draw_feats(jax.random.fold_in(key_of[7], 71), 0),
        "row_map": draw_row_map(jax.random.fold_in(key_of[7], 71), 0),
        "clip_ids": jnp.searchsorted(jnp.cumsum(ragged(key_of[2], CLIPS, FRAMES, MOST, 0)), jnp.arange(FRAMES), side="right").astype(jnp.int32),
        "norm_gain": jnp.clip(1.0 + 0.18 * jax.random.normal(key_of[3], (C,), jnp.float32), 0.1, 1.9),
        "norm_bias": normal_values(key_of[4], (C,), 0.5, 3.0, jnp.float32),
        "conv_weight": normal_values(key_of[5], (3, 3, 3, C, C), (27 * C) ** -0.5, 0.0546875),
        "conv_bias": normal_values(key_of[6], (C,), 0.3, 2.0, jnp.float32),
    }


def reference(feats, row_map, clip_ids, norm_gain, norm_bias, conv_weight, conv_bias):
    placed = jnp.zeros_like(feats).at[row_map].set(feats)
    features = placed.reshape(N_SRC, N_FRAME, N_TILE, FR_DEV, HR, WCOL, C)
    features = features.transpose(1, 3, 2, 4, 0, 5, 6).reshape(FRAMES, HEIGHT, WIDTH, C)
    group_width = C // GROUPS
    shaped = features.reshape(FRAMES, HEIGHT * WIDTH, GROUPS, group_width)
    onehot = (clip_ids[:, None] == jnp.arange(CLIPS, dtype=jnp.int32)[None, :]).astype(jnp.float32)
    counts = lax.optimization_barrier(jnp.sum(onehot, axis=0)) * (HEIGHT * WIDTH * group_width)
    frame_sum = lax.optimization_barrier(jnp.sum(shaped, axis=(1, 3)))
    clip_mean = jnp.dot(onehot.T, frame_sum, precision=lax.Precision.HIGHEST) / counts[:, None]
    frame_mean = jnp.dot(onehot, clip_mean, precision=lax.Precision.HIGHEST)
    centred = shaped - frame_mean[:, None, :, None]
    frame_sq = lax.optimization_barrier(jnp.sum(centred * centred, axis=(1, 3)))
    clip_var = jnp.dot(onehot.T, frame_sq, precision=lax.Precision.HIGHEST) / counts[:, None]
    inverse_std = 1.0 / jnp.sqrt(clip_var + 1e-06)
    frame_inv = jnp.dot(onehot, inverse_std, precision=lax.Precision.HIGHEST)
    normed = (centred * frame_inv[:, None, :, None]).reshape(FRAMES, HEIGHT, WIDTH, C)
    activated = jax.nn.silu(normed * norm_gain + norm_bias).astype(jnp.bfloat16)
    act_wide = activated.astype(jnp.float32)
    kernel = conv_weight.astype(jnp.float32)
    conv_sum = jnp.zeros((FRAMES, HEIGHT, WIDTH, C), jnp.float32)
    for tap_time in range(3):
        delay_steps = 2 - tap_time
        if delay_steps > 0:
            shifted = jnp.concatenate([jnp.zeros((delay_steps, HEIGHT, WIDTH, C), jnp.float32), act_wide[:FRAMES - delay_steps]], axis=0)
            validity = jnp.concatenate([jnp.zeros((delay_steps,), jnp.float32), (clip_ids[delay_steps:] == clip_ids[:FRAMES - delay_steps]).astype(jnp.float32)])
        else:
            shifted = act_wide
            validity = jnp.ones((FRAMES,), jnp.float32)
        partial_value = lax.conv_general_dilated(shifted, kernel[tap_time], (1, 1), ((1, 1), (1, 1)), dimension_numbers=('NHWC', 'HWIO', 'NHWC'), precision=lax.Precision.HIGHEST)
        conv_sum = conv_sum + partial_value * validity[:, None, None, None]
    return (features + conv_sum + conv_bias).astype(jnp.bfloat16)
```

```python
import functools

import jax
import jax.numpy as jnp
from jax import lax
from jax.experimental import pallas as pl
from jax.experimental.pallas import tpu as pltpu
from jax.sharding import PartitionSpec as P

GROUPS = 32
CLIPS = 4
FR_DEV = 6
HR = 8
WCOL = 32
MESH = pl.DeviceIdType.MESH
BF = jnp.bfloat16
CODE = jnp.int16
STEPS = 1024.0
LOWEST = 26.6


F32 = jnp.float32
VMEM_LIMIT = 56 * 1024 * 1024


def dot(a, b):
    return jnp.dot(a, b, preferred_element_type=F32)


def dot_exact(a, b):
    return jnp.dot(a, b, preferred_element_type=F32, precision=lax.Precision.HIGHEST)


def iota(shape, dim):
    return lax.broadcasted_iota(jnp.int32, shape, dim)


def encode(x):
    octave = jnp.log2(jnp.maximum(jnp.abs(x), 1e-30)) + LOWEST
    code = jnp.clip(octave * STEPS + 0.5, 0.0, 32767.0).astype(jnp.int32)
    return jnp.where(x < 0.0, -code, code).astype(CODE)


def decode(code):
    code = code.astype(jnp.int32).astype(F32)
    size = jnp.abs(code)
    value = jnp.exp2(size * (1.0 / STEPS) - LOWEST)
    value = jnp.where(size < 1.0, 0.0, value)
    return jnp.where(code < 0.0, -value, value)


def split3(x):
    hi = x.astype(BF)
    rest = x - hi.astype(F32)
    mid = rest.astype(BF)
    low = (rest - mid.astype(F32)).astype(BF)
    return hi, mid, low


def group_matrix(channels, width):
    return (iota((channels, 128), 0) // width == iota((channels, 128), 1) % GROUPS).astype(F32)


def group_matrix_t(channels, width):
    return (iota((128, channels), 1) // width == iota((128, channels), 0) % GROUPS).astype(F32)


def clip_lanes():
    return iota((8, 128), 1) // GROUPS == iota((8, 128), 0)


def reshard_kernel(sizes, block, info_ref, feats_ref, arrived_ref, msgs_ref, packed, msg,
                   send_sem, recv_sem, msend_sem, mrecv_sem):
    n_src, n_frame, n_tile = sizes
    devices = n_src * n_frame * n_tile
    rows, channels = feats_ref.shape
    width = channels // GROUPS
    me = (lax.axis_index("src") * n_frame + lax.axis_index("frame")) * n_tile + lax.axis_index("tile")

    def coords(k):
        peer = lax.rem(me + k, devices)
        return (peer // (n_frame * n_tile), lax.rem(peer // n_tile, n_frame), lax.rem(peer, n_tile))

    barrier = pltpu.get_barrier_semaphore()

    def greet(k, carry):
        pl.semaphore_signal(barrier, inc=1, device_id=coords(k), device_id_type=MESH)
        return carry

    lax.fori_loop(1, devices, greet, 0)

    owner = info_ref[0:1, :]
    slot_hi = info_ref[1:2, :].astype(F32)
    slot_lo = info_ref[2:3, :].astype(F32)
    clip = info_ref[3:4, :]

    owner_is = iota((devices, rows), 0) == owner
    onehot = owner_is.astype(F32)
    onehot_b = onehot.astype(BF)
    span = 256
    before = (iota((span, span), 0) < iota((span, span), 1)).astype(F32).astype(BF)
    running = jnp.zeros((devices, 1), F32)
    ranks = []
    for start in range(0, rows, span):
        part = onehot[:, start : start + span]
        ahead = dot(onehot_b[:, start : start + span], before) + running
        ranks.append(jnp.sum(part * ahead, axis=0, keepdims=True))
        running = running + jnp.sum(part, axis=1, keepdims=True)
    rank = jnp.concatenate(ranks, axis=1).astype(jnp.int32)
    position = owner * block + rank
    hi, mid, low = split3(feats_ref[...])
    total = devices * block
    chunk = total // 4
    for start in range(0, total, chunk):
        pick = (iota((chunk, rows), 0) + start == position).astype(F32).astype(BF)
        packed[pl.ds(start, chunk), :] = encode(dot(pick, hi) + dot(pick, mid))

    pl.semaphore_wait(barrier, devices - 1)

    def row_copy(k):
        return pltpu.make_async_remote_copy(
            src_ref=packed.at[pl.ds(pl.multiple_of(k * block, 16), block)],
            dst_ref=arrived_ref.at[pl.ds(pl.multiple_of(me * block, 16), block)],
            send_sem=send_sem.at[k],
            recv_sem=recv_sem.at[k],
            device_id=coords(k),
            device_id_type=MESH,
        )

    def send_rows(k, carry):
        row_copy(k).start()
        return carry

    lax.fori_loop(1, devices, send_rows, 0)
    arrived_ref[pl.ds(pl.multiple_of(me * block, 16), block), :] = packed[0:block, :]

    rank_is = (iota((128, rows), 0) == rank).astype(F32).astype(BF)
    contract = (((1,), (1,)), ((), ()))
    ids = 32.0 * lax.dot_general(
        (onehot * slot_hi).astype(BF), rank_is, contract, preferred_element_type=F32
    ) + lax.dot_general((onehot * slot_lo).astype(BF), rank_is, contract, preferred_element_type=F32)

    in_clip = (iota((8, rows), 0) == clip).astype(F32)
    in_clip_b = in_clip.astype(BF)
    counts = jnp.sum(in_clip, axis=1, keepdims=True) * float(width)
    sums = dot(in_clip_b, hi) + dot(in_clip_b, mid) + dot(in_clip_b, low)
    to_groups = group_matrix(channels, width)
    group_sums = dot_exact(sums, to_groups)
    own_lanes = clip_lanes()
    means = jnp.where(iota((8, 128), 1) < GROUPS, group_sums / jnp.maximum(counts, 1.0), 0.0)
    m_hi, m_mid, m_low = split3(dot_exact(means, group_matrix_t(channels, width)))
    by_row = in_clip.T.astype(BF)
    centre = dot(by_row, m_hi) + dot(by_row, m_mid) + dot(by_row, m_low)
    centred = feats_ref[...] - centre
    s_hi, s_mid, s_low = split3(centred * centred)
    squares = dot(in_clip_b, s_hi) + dot(in_clip_b, s_mid) + dot(in_clip_b, s_low)
    group_squares = dot_exact(squares, to_groups)

    def lanes(x):
        return jnp.sum(jnp.where(own_lanes, x, 0.0), axis=0, keepdims=True)

    line = iota((8, 128), 0)
    stats = jnp.where(
        line == 1,
        lanes(group_sums),
        jnp.where(line == 2, lanes(group_squares),
                  jnp.where(line == 3, lanes(jnp.broadcast_to(counts, (8, 128))), 0.0)),
    )
    wide = (devices, 8, 128)
    msg[...] = jnp.where(
        iota(wide, 1) == 0,
        jnp.broadcast_to(ids[:, None, :], wide),
        jnp.broadcast_to(stats[None], wide),
    )

    def msg_copy(k):
        return pltpu.make_async_remote_copy(
            src_ref=msg.at[k],
            dst_ref=msgs_ref.at[me],
            send_sem=msend_sem.at[k],
            recv_sem=mrecv_sem.at[k],
            device_id=coords(k),
            device_id_type=MESH,
        )

    def send_msg(k, carry):
        msg_copy(k).start()
        return carry

    lax.fori_loop(1, devices, send_msg, 0)
    msgs_ref[pl.ds(me, 1)] = msg[0:1]

    def finish(k, carry):
        row_copy(k).wait()
        msg_copy(k).wait()
        return carry

    lax.fori_loop(1, devices, finish, 0)


def place_kernel(clips_ref, targets_ref, msgs_ref, arrived_ref, gain_ref, bias_ref,
                 features_ref, act_ref, first_ref, last_ref, mean_s, inv_s):
    rows, channels = features_ref.shape
    width = channels // GROUPS
    sums = msgs_ref[:, 1, :]
    squares = msgs_ref[:, 2, :]
    counts = msgs_ref[:, 3, :]
    total = jnp.sum(counts, axis=0, keepdims=True)
    mean = jnp.sum(sums, axis=0, keepdims=True) / total
    off = sums / jnp.maximum(counts, 1.0) - mean
    var = jnp.sum(squares + counts * (off * off), axis=0, keepdims=True) / total
    inv = 1.0 / jnp.sqrt(var + 1e-06)
    spread = group_matrix_t(channels, width)
    own_lanes = clip_lanes()
    mean_s[...] = dot_exact(jnp.where(own_lanes, mean, 0.0), spread)
    inv_s[...] = dot_exact(jnp.where(own_lanes, inv, 0.0), spread)
    first_frame = lax.axis_index("frame") * FR_DEV
    plane = HR * WCOL
    first_ref[...] = jnp.zeros_like(first_ref)
    last_ref[...] = jnp.zeros_like(last_ref)
    arrived = decode(arrived_ref[...])
    hi = arrived.astype(BF)
    rest = (arrived - hi.astype(F32)).astype(BF)
    for t in range(FR_DEV):
        pick = (iota((plane, targets_ref.shape[1]), 0) + t * plane == targets_ref[...]).astype(F32).astype(BF)
        x = dot(pick, hi) + dot(pick, rest)
        features_ref[pl.ds(t * plane, plane), :] = x
        c = clips_ref[first_frame + t]
        normed = (x - mean_s[pl.ds(c, 1), :]) * inv_s[pl.ds(c, 1), :]
        v = normed * gain_ref[...] + bias_ref[...]
        act = v / (1.0 + jnp.exp(-v))
        for h in range(HR):
            slab = act[h * WCOL : (h + 1) * WCOL]
            act_ref[t, h] = slab.astype(BF)
            rounded = slab.astype(BF).astype(F32)
            first_ref[h, t : t + 1, :] = rounded[0:1]
            last_ref[h, t : t + 1, :] = rounded[WCOL - 1 : WCOL]


def halo_kernel(sizes, act_ref, first_ref, last_ref, x_ref, cl_ref, cr_ref, own_sem, send_sem, recv_sem):
    n_src, n_frame, n_tile = sizes
    s, f, t = lax.axis_index("src"), lax.axis_index("frame"), lax.axis_index("tile")
    x_ref[0:2] = jnp.zeros_like(x_ref[0:2])
    for edge in (0, HR + 1):
        x_ref[2:, edge] = jnp.zeros_like(x_ref[2:, edge])
    cl_ref[...] = jnp.zeros_like(cl_ref)
    cr_ref[...] = jnp.zeros_like(cr_ref)

    moves = [(ds, df, dt) for df in (0, 1) for dt in (0, -1, 1) for ds in (0, -1, 1)][1:]

    def inside(ds, df, dt):
        return ((s + ds >= 0) & (s + ds < n_src) & (f + df >= 0) & (f + df < n_frame)
                & (t + dt >= 0) & (t + dt < n_tile))

    barrier = pltpu.get_barrier_semaphore()
    heard = jnp.int32(0)
    for ds, df, dt in moves:
        @pl.when(inside(-ds, -df, -dt))
        def _():
            pl.semaphore_signal(barrier, inc=1, device_id=(s - ds, f - df, t - dt), device_id_type=MESH)

        heard = heard + inside(ds, df, dt).astype(jnp.int32)
    pl.semaphore_wait(barrier, heard)

    def copy(i, move):
        ds, df, dt = move
        from_h, to_h, count = {0: (0, 1, HR), 1: (HR - 1, 0, 1), -1: (0, HR + 1, 1)}[dt]
        if ds == 0:
            from_t, to_t, frames = (0, 2, FR_DEV) if df == 0 else (FR_DEV - 2, 0, 2)
            src = act_ref.at[pl.ds(from_t, frames), pl.ds(from_h, count)]
            dst = x_ref.at[pl.ds(to_t, frames), pl.ds(to_h, count)]
        else:
            src = (last_ref if ds == 1 else first_ref).at[pl.ds(from_h, count)]
            dst = (cl_ref if ds == 1 else cr_ref).at[df, pl.ds(to_h, count)]
        return pltpu.make_async_remote_copy(
            src_ref=src, dst_ref=dst, send_sem=send_sem.at[i], recv_sem=recv_sem.at[i],
            device_id=(s + ds, f + df, t + dt), device_id_type=MESH,
        )

    for i, move in enumerate(moves):
        @pl.when(inside(*move))
        def _(i=i, move=move):
            copy(i, move).start()
    own = pltpu.make_async_copy(act_ref, x_ref.at[pl.ds(2, FR_DEV), pl.ds(1, HR)], own_sem)
    own.start()
    own.wait()
    for i, move in enumerate(moves):
        @pl.when(inside(*move))
        def _(i=i, move=move):
            copy(i, move).wait_send()

        @pl.when(inside(-move[0], -move[1], -move[2]))
        def _(i=i, move=move):
            copy(i, move).wait_recv()


def conv_kernel(clips_ref, x_ref, cl_ref, cr_ref, w_ref, features_ref, bias_ref, out_ref, xs, acc):
    step = pl.program_id(0)
    channels = x_ref.shape[-1]
    plane = HR * WCOL
    first_frame = lax.axis_index("frame") * FR_DEV
    a, b = step // 3, step % 3

    @pl.when(step == 0)
    def _():
        row = iota((WCOL, channels), 0)

        def widen(h, carry):
            for t in range(FR_DEV + 2):
                here = x_ref[t, h]
                wide = here.astype(F32)
                part, line = (1, FR_DEV - 2 + t) if t < 2 else (0, t - 2)
                left = cl_ref[part, h][line : line + 1]
                right = cr_ref[part, h][line : line + 1]
                xs[t, h, :, 0:channels] = jnp.where(row == 0, left, pltpu.roll(wide, 1, 0)).astype(BF)
                xs[t, h, :, channels : 2 * channels] = here
                xs[t, h, :, 2 * channels :] = jnp.where(
                    row == WCOL - 1, right, pltpu.roll(wide, WCOL - 1, 0)
                ).astype(BF)
            return carry

        lax.fori_loop(0, HR + 2, widen, 0)
        acc[...] = jnp.zeros_like(acc)

    for t in range(0, FR_DEV, 2):
        lhs = xs[pl.ds(a + t, 2), pl.ds(b, HR)].reshape(2 * plane, 3 * channels)
        part = dot(lhs, w_ref[0])
        for u in range(2):
            frame = first_frame + t + u
            source = frame - 2 + a
            same = (source >= 0) & (clips_ref[jnp.maximum(source, 0)] == clips_ref[frame])
            at = pl.ds((t + u) * plane, plane)
            acc[at, :] += jnp.where(same, part[u * plane : (u + 1) * plane], 0.0)

    @pl.when(step == 8)
    def _():
        for t in range(FR_DEV):
            at = pl.ds(t * plane, plane)
            y = features_ref[at, :] + acc[at, :] + bias_ref[...]
            out_ref[t] = y.astype(BF).reshape(HR, WCOL, channels)


def shards(feats, row_map, clip_ids, norm_gain, norm_bias, conv_weight, conv_bias):
    rows, channels = feats.shape
    sizes = tuple(lax.axis_size(name) for name in ("src", "frame", "tile"))
    n_src, n_frame, n_tile = sizes
    devices = n_src * n_frame * n_tile
    block = (rows // devices + 15) // 16 * 16
    me = (lax.axis_index("src") * n_frame + lax.axis_index("frame")) * n_tile + lax.axis_index("tile")
    owner = row_map // rows
    slot = row_map % rows
    frame = owner // n_tile % n_frame * FR_DEV + slot // (HR * WCOL)
    frames = jnp.arange(clip_ids.shape[0], dtype=jnp.int32)
    clip = jnp.sum(jnp.where(frames[:, None] == frame[None, :], clip_ids[:, None], 0), axis=0)
    info = jnp.stack([(owner - me) % devices, slot // 32, slot % 32, clip])
    vmem = pl.BlockSpec(memory_space=pltpu.VMEM)
    smem = pl.BlockSpec(memory_space=pltpu.SMEM)
    dma = pltpu.SemaphoreType.DMA
    arrived, msgs = pl.pallas_call(
        functools.partial(reshard_kernel, sizes, block),
        out_shape=(
            jax.ShapeDtypeStruct((devices * block, channels), CODE),
            jax.ShapeDtypeStruct((devices, 8, 128), F32),
        ),
        in_specs=[vmem] * 2,
        out_specs=(vmem, vmem),
        scratch_shapes=[
            pltpu.VMEM((devices * block, channels), CODE),
            pltpu.VMEM((devices, 8, 128), F32),
            dma((devices,)),
            dma((devices,)),
            dma((devices,)),
            dma((devices,)),
        ],
        compiler_params=pltpu.CompilerParams(
            collective_id=0, has_side_effects=True, vmem_limit_bytes=VMEM_LIMIT
        ),
        name="reshard",
    )(info, feats)
    targets = msgs[:, 0, :block].reshape(1, devices * block).astype(jnp.int32)
    edge = jax.ShapeDtypeStruct((HR, 8, channels), F32)
    features, act, first, last = pl.pallas_call(
        place_kernel,
        out_shape=(
            jax.ShapeDtypeStruct((rows, channels), F32),
            jax.ShapeDtypeStruct((FR_DEV, HR, WCOL, channels), BF),
            edge,
            edge,
        ),
        in_specs=[smem] + [vmem] * 5,
        out_specs=(vmem,) * 4,
        scratch_shapes=[pltpu.VMEM((8, channels), F32)] * 2,
        compiler_params=pltpu.CompilerParams(vmem_limit_bytes=VMEM_LIMIT),
        name="place",
    )(clip_ids, targets, msgs, arrived, norm_gain[None], norm_bias[None])
    beside = jax.ShapeDtypeStruct((2, HR + 2, 8, channels), F32)
    x, left, right = pl.pallas_call(
        functools.partial(halo_kernel, sizes),
        out_shape=(
            jax.ShapeDtypeStruct((FR_DEV + 2, HR + 2, WCOL, channels), BF),
            beside,
            beside,
        ),
        in_specs=[vmem] * 3,
        out_specs=(vmem,) * 3,
        scratch_shapes=[dma, dma((17,)), dma((17,))],
        compiler_params=pltpu.CompilerParams(
            collective_id=1, has_side_effects=True, vmem_limit_bytes=VMEM_LIMIT
        ),
        name="halo",
    )(act, first, last)
    whole = lambda *shape: pl.BlockSpec(shape, lambda i: (0,) * len(shape))
    return pl.pallas_call(
        conv_kernel,
        grid=(9,),
        out_shape=jax.ShapeDtypeStruct((FR_DEV, HR, WCOL, channels), BF),
        in_specs=[
            smem,
            vmem,
            vmem,
            vmem,
            pl.BlockSpec((1, 3 * channels, channels), lambda i: (i, 0, 0)),
            vmem,
            vmem,
        ],
        out_specs=whole(FR_DEV, HR, WCOL, channels),
        scratch_shapes=[
            pltpu.VMEM((FR_DEV + 2, HR + 2, WCOL, 3 * channels), BF),
            pltpu.VMEM((rows, channels), F32),
        ],
        compiler_params=pltpu.CompilerParams(vmem_limit_bytes=VMEM_LIMIT),
        name="conv",
    )(clip_ids, x, left, right, conv_weight.reshape(9, 3 * channels, channels), features, conv_bias[None])


def solution(mesh):
    placed = (
        P(("src", "frame", "tile"), None),
        P(("src", "frame", "tile")),
        P(),
        P(),
        P(),
        P(),
        P(),
    )
    return jax.shard_map(
        shards,
        mesh=mesh,
        in_specs=placed,
        out_specs=P("frame", "tile", "src", None),
        check_vma=False,
    )
```

```python
import functools

import jax
import jax.numpy as jnp
from jax import lax
from jax.experimental import pallas as pl
from jax.experimental.pallas import tpu as pltpu
from jax.sharding import PartitionSpec as P

GROUPS = 32
CLIPS = 4
FR_DEV = 6
HR = 8
WCOL = 32
MESH = pl.DeviceIdType.MESH
BF = jnp.bfloat16
CODE = jnp.int16
STEPS = 1024.0
LOWEST = 26.6


F32 = jnp.float32
VMEM_LIMIT = 56 * 1024 * 1024


def dot(a, b):
    return jnp.dot(a, b, preferred_element_type=F32)


def dot_exact(a, b):
    return jnp.dot(a, b, preferred_element_type=F32, precision=lax.Precision.HIGHEST)


def iota(shape, dim):
    return lax.broadcasted_iota(jnp.int32, shape, dim)


def encode(x):
    octave = jnp.log2(jnp.maximum(jnp.abs(x), 1e-30)) + LOWEST
    code = jnp.clip(octave * STEPS + 0.5, 0.0, 32767.0).astype(jnp.int32)
    return jnp.where(x < 0.0, -code, code).astype(CODE)


def decode(code):
    code = code.astype(jnp.int32).astype(F32)
    size = jnp.abs(code)
    value = jnp.exp2(size * (1.0 / STEPS) - LOWEST)
    value = jnp.where(size < 1.0, 0.0, value)
    return jnp.where(code < 0.0, -value, value)


def split3(x):
    hi = x.astype(BF)
    rest = x - hi.astype(F32)
    mid = rest.astype(BF)
    low = (rest - mid.astype(F32)).astype(BF)
    return hi, mid, low


def group_matrix(channels, width):
    return (iota((channels, 128), 0) // width == iota((channels, 128), 1) % GROUPS).astype(F32)


def group_matrix_t(channels, width):
    return (iota((128, channels), 1) // width == iota((128, channels), 0) % GROUPS).astype(F32)


def clip_lanes():
    return iota((8, 128), 1) // GROUPS == iota((8, 128), 0)


def reshard_kernel(sizes, block, info_ref, feats_ref, arrived_ref, msgs_ref, packed, msg,
                   send_sem, recv_sem, msend_sem, mrecv_sem):
    n_src, n_frame, n_tile = sizes
    devices = n_src * n_frame * n_tile
    rows, channels = feats_ref.shape
    width = channels // GROUPS
    me = (lax.axis_index("src") * n_frame + lax.axis_index("frame")) * n_tile + lax.axis_index("tile")

    def coords(k):
        peer = lax.rem(me + k, devices)
        return (peer // (n_frame * n_tile), lax.rem(peer // n_tile, n_frame), lax.rem(peer, n_tile))

    barrier = pltpu.get_barrier_semaphore()

    def greet(k, carry):
        pl.semaphore_signal(barrier, inc=1, device_id=coords(k), device_id_type=MESH)
        return carry

    lax.fori_loop(1, devices, greet, 0)

    owner = info_ref[0:1, :]
    slot_hi = info_ref[1:2, :].astype(F32)
    slot_lo = info_ref[2:3, :].astype(F32)
    clip = info_ref[3:4, :]

    owner_is = iota((devices, rows), 0) == owner
    onehot = owner_is.astype(F32)
    onehot_b = onehot.astype(BF)
    span = 256
    before = (iota((span, span), 0) < iota((span, span), 1)).astype(F32).astype(BF)
    running = jnp.zeros((devices, 1), F32)
    ranks = []
    for start in range(0, rows, span):
        part = onehot[:, start : start + span]
        ahead = dot(onehot_b[:, start : start + span], before) + running
        ranks.append(jnp.sum(part * ahead, axis=0, keepdims=True))
        running = running + jnp.sum(part, axis=1, keepdims=True)
    rank = jnp.concatenate(ranks, axis=1).astype(jnp.int32)
    position = owner * block + rank
    hi, mid, low = split3(feats_ref[...])
    total = devices * block
    chunk = total // 4
    for start in range(0, total, chunk):
        pick = (iota((chunk, rows), 0) + start == position).astype(F32).astype(BF)
        packed[pl.ds(start, chunk), :] = encode(dot(pick, hi) + dot(pick, mid))

    pl.semaphore_wait(barrier, devices - 1)

    def row_copy(k):
        return pltpu.make_async_remote_copy(
            src_ref=packed.at[pl.ds(pl.multiple_of(k * block, 16), block)],
            dst_ref=arrived_ref.at[pl.ds(pl.multiple_of(me * block, 16), block)],
            send_sem=send_sem.at[k],
            recv_sem=recv_sem.at[k],
            device_id=coords(k),
            device_id_type=MESH,
        )

    def send_rows(k, carry):
        row_copy(k).start()
        return carry

    lax.fori_loop(1, devices, send_rows, 0)
    arrived_ref[pl.ds(pl.multiple_of(me * block, 16), block), :] = packed[0:block, :]

    rank_is = (iota((128, rows), 0) == rank).astype(F32).astype(BF)
    contract = (((1,), (1,)), ((), ()))
    ids = 32.0 * lax.dot_general(
        (onehot * slot_hi).astype(BF), rank_is, contract, preferred_element_type=F32
    ) + lax.dot_general((onehot * slot_lo).astype(BF), rank_is, contract, preferred_element_type=F32)

    in_clip = (iota((8, rows), 0) == clip).astype(F32)
    in_clip_b = in_clip.astype(BF)
    counts = jnp.sum(in_clip, axis=1, keepdims=True) * float(width)
    sums = dot(in_clip_b, hi) + dot(in_clip_b, mid) + dot(in_clip_b, low)
    to_groups = group_matrix(channels, width)
    group_sums = dot_exact(sums, to_groups)
    own_lanes = clip_lanes()
    means = jnp.where(iota((8, 128), 1) < GROUPS, group_sums / jnp.maximum(counts, 1.0), 0.0)
    m_hi, m_mid, m_low = split3(dot_exact(means, group_matrix_t(channels, width)))
    by_row = in_clip.T.astype(BF)
    centre = dot(by_row, m_hi) + dot(by_row, m_mid) + dot(by_row, m_low)
    centred = feats_ref[...] - centre
    s_hi, s_mid, s_low = split3(centred * centred)
    squares = dot(in_clip_b, s_hi) + dot(in_clip_b, s_mid) + dot(in_clip_b, s_low)
    group_squares = dot_exact(squares, to_groups)

    def lanes(x):
        return jnp.sum(jnp.where(own_lanes, x, 0.0), axis=0, keepdims=True)

    line = iota((8, 128), 0)
    stats = jnp.where(
        line == 1,
        lanes(group_sums),
        jnp.where(line == 2, lanes(group_squares),
                  jnp.where(line == 3, lanes(jnp.broadcast_to(counts, (8, 128))), 0.0)),
    )
    wide = (devices, 8, 128)
    msg[...] = jnp.where(
        iota(wide, 1) == 0,
        jnp.broadcast_to(ids[:, None, :], wide),
        jnp.broadcast_to(stats[None], wide),
    )

    def msg_copy(k):
        return pltpu.make_async_remote_copy(
            src_ref=msg.at[k],
            dst_ref=msgs_ref.at[me],
            send_sem=msend_sem.at[k],
            recv_sem=mrecv_sem.at[k],
            device_id=coords(k),
            device_id_type=MESH,
        )

    def send_msg(k, carry):
        msg_copy(k).start()
        return carry

    lax.fori_loop(1, devices, send_msg, 0)
    msgs_ref[pl.ds(me, 1)] = msg[0:1]

    def finish(k, carry):
        row_copy(k).wait()
        msg_copy(k).wait()
        return carry

    lax.fori_loop(1, devices, finish, 0)


def place_kernel(clips_ref, targets_ref, msgs_ref, arrived_ref, gain_ref, bias_ref,
                 features_ref, act_ref, first_ref, last_ref, firstp_ref, lastp_ref, mean_s, inv_s):
    rows, channels = features_ref.shape
    width = channels // GROUPS
    sums = msgs_ref[:, 1, :]
    squares = msgs_ref[:, 2, :]
    counts = msgs_ref[:, 3, :]
    total = jnp.sum(counts, axis=0, keepdims=True)
    mean = jnp.sum(sums, axis=0, keepdims=True) / total
    off = sums / jnp.maximum(counts, 1.0) - mean
    var = jnp.sum(squares + counts * (off * off), axis=0, keepdims=True) / total
    inv = 1.0 / jnp.sqrt(var + 1e-06)
    spread = group_matrix_t(channels, width)
    own_lanes = clip_lanes()
    mean_s[...] = dot_exact(jnp.where(own_lanes, mean, 0.0), spread)
    inv_s[...] = dot_exact(jnp.where(own_lanes, inv, 0.0), spread)
    first_frame = lax.axis_index("frame") * FR_DEV
    plane = HR * WCOL
    first_ref[...] = jnp.zeros_like(first_ref)
    last_ref[...] = jnp.zeros_like(last_ref)
    arrived = decode(arrived_ref[...])
    hi = arrived.astype(BF)
    rest = (arrived - hi.astype(F32)).astype(BF)
    for t in range(FR_DEV):
        pick = (iota((plane, targets_ref.shape[1]), 0) + t * plane == targets_ref[...]).astype(F32).astype(BF)
        x = dot(pick, hi) + dot(pick, rest)
        features_ref[pl.ds(t * plane, plane), :] = x
        c = clips_ref[first_frame + t]
        normed = (x - mean_s[pl.ds(c, 1), :]) * inv_s[pl.ds(c, 1), :]
        v = normed * gain_ref[...] + bias_ref[...]
        act = v / (1.0 + jnp.exp(-v))
        for h in range(HR):
            slab = act[h * WCOL : (h + 1) * WCOL]
            act_ref[t, h] = slab.astype(BF)
            rounded = slab.astype(BF).astype(F32)
            first_ref[h, t : t + 1, :] = rounded[0:1]
            last_ref[h, t : t + 1, :] = rounded[WCOL - 1 : WCOL]
            if t >= FR_DEV - 2:
                u = t - (FR_DEV - 2)
                firstp_ref[u, h : h + 1, :] = rounded[0:1]
                lastp_ref[u, h : h + 1, :] = rounded[WCOL - 1 : WCOL]


def decode_kernel(sizes, clips_ref, act_ref, first_ref, last_ref, firstp_ref, lastp_ref, features_ref, bias_ref,
                  w_ref, out_ref, xs, acc, weights, prev, edge, col, corner, colp, cornerp,
                  w_sem, send_sem, recv_sem):
    n_src, n_frame, n_tile = sizes
    s, f, t = lax.axis_index("src"), lax.axis_index("frame"), lax.axis_index("tile")
    channels = act_ref.shape[-1]
    plane = HR * WCOL

    def weight_copy(i):
        return pltpu.make_async_copy(w_ref.at[i], weights.at[i], w_sem.at[i])

    taps_order = [1, 4, 7, 0, 3, 6, 2, 5, 8]
    for i in taps_order:
        weight_copy(i).start()
    for ref in (prev, edge, col, corner, colp, cornerp):
        ref[...] = jnp.zeros_like(ref)

    moves = [(ds, 0, 0) for ds in (-1, 1)]
    moves += [(0, 1, 0)]
    moves += [(ds, 0, dt) for dt in (-1, 1) for ds in (0, -1, 1)]
    moves += [(ds, 1, dt) for dt in (0, -1, 1) for ds in (0, -1, 1)][1:]

    def inside(ds, df, dt):
        return ((s + ds >= 0) & (s + ds < n_src) & (f + df >= 0) & (f + df < n_frame)
                & (t + dt >= 0) & (t + dt < n_tile))

    barrier = pltpu.get_barrier_semaphore()
    heard = jnp.int32(0)
    for ds, df, dt in moves:
        @pl.when(inside(-ds, -df, -dt))
        def _():
            pl.semaphore_signal(barrier, inc=1, device_id=(s - ds, f - df, t - dt), device_id_type=MESH)

        heard = heard + inside(ds, df, dt).astype(jnp.int32)

    for u in range(FR_DEV):
        at = pl.ds(u * plane, plane)
        acc[at, :] = features_ref[at, :] + bias_ref[...]
    pl.semaphore_wait(barrier, heard)

    def copy(i, move):
        ds, df, dt = move
        row = HR - 1 if dt == 1 else 0
        end = 0 if dt == 1 else 1
        side = 0 if ds == 1 else 1
        if ds == 0 and df == 0:
            src, dst = act_ref.at[:, row], edge.at[end]
        elif ds == 0:
            src = act_ref.at[pl.ds(FR_DEV - 2, 2), pl.ds(0, HR)] if dt == 0 else act_ref.at[pl.ds(FR_DEV - 2, 2), row]
            dst = prev.at[:, pl.ds(1, HR)] if dt == 0 else prev.at[:, (HR + 1) * end]
        elif df == 0:
            ref = last_ref if ds == 1 else first_ref
            src, dst = (ref, col.at[side]) if dt == 0 else (ref.at[row], corner.at[side, end])
        else:
            if dt == 0:
                src, dst = lastp_ref if ds == 1 else firstp_ref, colp.at[side]
            else:
                src, dst = (last_ref if ds == 1 else first_ref).at[row], cornerp.at[side, end]
        return pltpu.make_async_remote_copy(
            src_ref=src, dst_ref=dst, send_sem=send_sem.at[i], recv_sem=recv_sem.at[i],
            device_id=(s + ds, f + df, t + dt), device_id_type=MESH,
        )

    for i, move in enumerate(moves):
        @pl.when(inside(*move))
        def _(i=i, move=move):
            copy(i, move).start()

    def arrive(lo, hi):
        for i, move in list(enumerate(moves))[lo:hi]:
            @pl.when(inside(-move[0], -move[1], -move[2]))
            def _(i=i, move=move):
                copy(i, move).wait_recv()

    first_frame = f * FR_DEV

    def add(part, a, lo):
        for j in range(part.shape[0] // plane):
            here = part[j * plane : (j + 1) * plane]
            at = pl.ds((lo + j) * plane, plane)
            if a < 2:
                frame = first_frame + lo + j
                source = frame - 2 + a
                same = (source >= 0) & (clips_ref[jnp.maximum(source, 0)] == clips_ref[frame])
                here = jnp.where(same, here, 0.0)
            acc[at, :] += here

    groups = [(2, 0, 3), (2, 3, 3), (1, 1, 3), (1, 4, 2), (0, 2, 2), (0, 4, 2)]
    mid_lanes = slice(channels, 2 * channels)
    for a, lo, n in groups:
        if lo in (0, 1, 2):
            weight_copy(3 * a + 1).wait()
        u = lo - 2 + a
        lhs = act_ref[u : u + n].reshape(n * plane, channels)
        add(dot(lhs, weights[3 * a + 1, mid_lanes]), a, lo)

    rows32 = iota((WCOL, channels), 0)

    def widen(u, h, here, left, right):
        wide = here.astype(F32)
        xs[u, h, :, 0:channels] = jnp.where(rows32 == 0, left, pltpu.roll(wide, 1, 0)).astype(BF)
        xs[u, h, :, channels : 2 * channels] = here
        xs[u, h, :, 2 * channels :] = jnp.where(
            rows32 == WCOL - 1, right, pltpu.roll(wide, WCOL - 1, 0)
        ).astype(BF)

    arrive(0, 2)

    def widen_own(h, carry):
        for u in range(FR_DEV):
            widen(u + 2, h + 1, act_ref[u, h], col[0, h, u : u + 1], col[1, h, u : u + 1])
        return carry

    lax.fori_loop(0, HR, widen_own, 0)

    def taken(u, n, b, lanes):
        return xs[u : u + n, b : b + HR, :, lanes].reshape(n * plane, -1)

    for a, lo, n in groups:
        u = lo + a
        w = weights.at[3 * a + 1]
        part = dot(taken(u, n, 1, slice(0, channels)), w[0:channels])
        part = part + dot(taken(u, n, 1, slice(2 * channels, 3 * channels)), w[2 * channels : 3 * channels])
        add(part, a, lo)

    arrive(3, 9)
    for end, h in ((0, 0), (1, HR + 1)):
        for u in range(FR_DEV):
            widen(u + 2, h, edge[end, u], corner[0, end, u : u + 1], corner[1, end, u : u + 1])
    for i in (0, 3, 6, 2, 5, 8):
        weight_copy(i).wait()
    every = slice(0, 3 * channels)
    for a, lo, n in groups:
        u = lo + a
        part = dot(taken(u, n, 0, every), weights[3 * a]) + dot(taken(u, n, 2, every), weights[3 * a + 2])
        add(part, a, lo)

    arrive(2, 3)
    arrive(9, len(moves))
    for u in range(2):
        line = FR_DEV - 2 + u
        for h in range(HR + 2):
            if 0 < h < HR + 1:
                left, right = colp[0, u, h - 1 : h], colp[1, u, h - 1 : h]
            else:
                end = h // (HR + 1)
                left, right = cornerp[0, end, line : line + 1], cornerp[1, end, line : line + 1]
            widen(u, h, prev[u, h], left, right)
    for a, n in ((0, 2), (1, 1)):
        part = dot(taken(a, n, 0, every), weights[3 * a])
        part = part + dot(taken(a, n, 1, every), weights[3 * a + 1])
        part = part + dot(taken(a, n, 2, every), weights[3 * a + 2])
        add(part, a, 0)
    for u in range(FR_DEV):
        out_ref[u] = acc[pl.ds(u * plane, plane), :].astype(BF).reshape(HR, WCOL, channels)
    for i, move in enumerate(moves):
        @pl.when(inside(*move))
        def _(i=i, move=move):
            copy(i, move).wait_send()


def shards(feats, row_map, clip_ids, norm_gain, norm_bias, conv_weight, conv_bias):
    rows, channels = feats.shape
    sizes = tuple(lax.axis_size(name) for name in ("src", "frame", "tile"))
    n_src, n_frame, n_tile = sizes
    devices = n_src * n_frame * n_tile
    block = (rows // devices + 15) // 16 * 16
    me = (lax.axis_index("src") * n_frame + lax.axis_index("frame")) * n_tile + lax.axis_index("tile")
    owner = row_map // rows
    slot = row_map % rows
    frame = owner // n_tile % n_frame * FR_DEV + slot // (HR * WCOL)
    frames = jnp.arange(clip_ids.shape[0], dtype=jnp.int32)
    clip = jnp.sum(jnp.where(frames[:, None] == frame[None, :], clip_ids[:, None], 0), axis=0)
    info = jnp.stack([(owner - me) % devices, slot // 32, slot % 32, clip])
    vmem = pl.BlockSpec(memory_space=pltpu.VMEM)
    smem = pl.BlockSpec(memory_space=pltpu.SMEM)
    dma = pltpu.SemaphoreType.DMA
    arrived, msgs = pl.pallas_call(
        functools.partial(reshard_kernel, sizes, block),
        out_shape=(
            jax.ShapeDtypeStruct((devices * block, channels), CODE),
            jax.ShapeDtypeStruct((devices, 8, 128), F32),
        ),
        in_specs=[vmem] * 2,
        out_specs=(vmem, vmem),
        scratch_shapes=[
            pltpu.VMEM((devices * block, channels), CODE),
            pltpu.VMEM((devices, 8, 128), F32),
            dma((devices,)),
            dma((devices,)),
            dma((devices,)),
            dma((devices,)),
        ],
        compiler_params=pltpu.CompilerParams(
            collective_id=0, has_side_effects=True, vmem_limit_bytes=VMEM_LIMIT
        ),
        name="reshard",
    )(info, feats)
    targets = msgs[:, 0, :block].reshape(1, devices * block).astype(jnp.int32)
    edge = jax.ShapeDtypeStruct((HR, 8, channels), F32)
    edge_p = jax.ShapeDtypeStruct((2, HR, channels), F32)
    features, act, first, last, firstp, lastp = pl.pallas_call(
        place_kernel,
        out_shape=(
            jax.ShapeDtypeStruct((rows, channels), F32),
            jax.ShapeDtypeStruct((FR_DEV, HR, WCOL, channels), BF),
            edge,
            edge,
            edge_p,
            edge_p,
        ),
        in_specs=[smem] + [vmem] * 5,
        out_specs=(vmem,) * 6,
        scratch_shapes=[pltpu.VMEM((8, channels), F32)] * 2,
        compiler_params=pltpu.CompilerParams(vmem_limit_bytes=VMEM_LIMIT),
        name="place",
    )(clip_ids, targets, msgs, arrived, norm_gain[None], norm_bias[None])
    return pl.pallas_call(
        functools.partial(decode_kernel, sizes),
        out_shape=jax.ShapeDtypeStruct((FR_DEV, HR, WCOL, channels), BF),
        in_specs=[smem] + [vmem] * 7 + [pl.BlockSpec(memory_space=pl.ANY)],
        out_specs=vmem,
        scratch_shapes=[
            pltpu.VMEM((FR_DEV + 2, HR + 2, WCOL, 3 * channels), BF),
            pltpu.VMEM((rows, channels), F32),
            pltpu.VMEM((9, 3 * channels, channels), BF),
            pltpu.VMEM((2, HR + 2, WCOL, channels), BF),
            pltpu.VMEM((2, FR_DEV, WCOL, channels), BF),
            pltpu.VMEM((2, HR, 8, channels), F32),
            pltpu.VMEM((2, 2, 8, channels), F32),
            pltpu.VMEM((2, 2, HR, channels), F32),
            pltpu.VMEM((2, 2, 8, channels), F32),
            dma((9,)),
            dma((17,)),
            dma((17,)),
        ],
        compiler_params=pltpu.CompilerParams(
            collective_id=1, has_side_effects=True, vmem_limit_bytes=VMEM_LIMIT
        ),
        name="halo_conv",
    )(clip_ids, act, first, last, firstp, lastp, features, conv_bias[None],
      conv_weight.reshape(9, 3 * channels, channels))


def solution(mesh):
    placed = (
        P(("src", "frame", "tile"), None),
        P(("src", "frame", "tile")),
        P(),
        P(),
        P(),
        P(),
        P(),
    )
    return jax.shard_map(
        shards,
        mesh=mesh,
        in_specs=placed,
        out_specs=P("frame", "tile", "src", None),
        check_vma=False,
    )
```

```python
import functools

import jax
import jax.numpy as jnp
from jax import lax
from jax.experimental import pallas as pl
from jax.experimental.pallas import tpu as pltpu
from jax.sharding import PartitionSpec as P

GROUPS = 32
CLIPS = 4
FR_DEV = 6
HR = 8
WCOL = 32
MESH = pl.DeviceIdType.MESH
BF = jnp.bfloat16
CODE = jnp.int16
STEPS = 1024.0
LOWEST = 26.6


F32 = jnp.float32
VMEM_LIMIT = 56 * 1024 * 1024


def dot(a, b):
    return jnp.dot(a, b, preferred_element_type=F32)


def dot_exact(a, b):
    return jnp.dot(a, b, preferred_element_type=F32, precision=lax.Precision.HIGHEST)


def iota(shape, dim):
    return lax.broadcasted_iota(jnp.int32, shape, dim)


def encode(x):
    octave = jnp.log2(jnp.maximum(jnp.abs(x), 1e-30)) + LOWEST
    code = jnp.clip(octave * STEPS + 0.5, 0.0, 32767.0).astype(jnp.int32)
    return jnp.where(x < 0.0, -code, code).astype(CODE)


def decode(code):
    code = code.astype(jnp.int32).astype(F32)
    size = jnp.abs(code)
    value = jnp.exp2(size * (1.0 / STEPS) - LOWEST)
    value = jnp.where(size < 1.0, 0.0, value)
    return jnp.where(code < 0.0, -value, value)


def split3(x):
    hi = x.astype(BF)
    rest = x - hi.astype(F32)
    mid = rest.astype(BF)
    low = (rest - mid.astype(F32)).astype(BF)
    return hi, mid, low


def group_matrix(channels, width):
    return (iota((channels, 128), 0) // width == iota((channels, 128), 1) % GROUPS).astype(F32)


def group_matrix_t(channels, width):
    return (iota((128, channels), 1) // width == iota((128, channels), 0) % GROUPS).astype(F32)


def clip_lanes():
    return iota((8, 128), 1) // GROUPS == iota((8, 128), 0)


def reshard_kernel(sizes, block, clips_ref, info_ref, feats_ref, gain_ref, bias_ref,
                   features_ref, act_ref, first_ref, last_ref, firstp_ref, lastp_ref,
                   packed, arrived, ids_out, ids_in, stats_out, stats_in,
                   send_sem, recv_sem, isend_sem, irecv_sem, ssend_sem, srecv_sem):
    n_src, n_frame, n_tile = sizes
    devices = n_src * n_frame * n_tile
    rows, channels = feats_ref.shape
    width = channels // GROUPS
    me = (lax.axis_index("src") * n_frame + lax.axis_index("frame")) * n_tile + lax.axis_index("tile")

    def coords(k):
        peer = lax.rem(me + k, devices)
        return (peer // (n_frame * n_tile), lax.rem(peer // n_tile, n_frame), lax.rem(peer, n_tile))

    barrier = pltpu.get_barrier_semaphore()

    def greet(k, carry):
        pl.semaphore_signal(barrier, inc=1, device_id=coords(k), device_id_type=MESH)
        return carry

    lax.fori_loop(1, devices, greet, 0)

    def row_copy(k):
        at = pl.ds(pl.multiple_of(k * block, 16), block)
        return pltpu.make_async_remote_copy(
            src_ref=packed.at[at], dst_ref=arrived.at[at],
            send_sem=send_sem.at[k], recv_sem=recv_sem.at[k],
            device_id=coords(k), device_id_type=MESH,
        )

    def ids_copy(k):
        return pltpu.make_async_remote_copy(
            src_ref=ids_out.at[k], dst_ref=ids_in.at[k],
            send_sem=isend_sem.at[k], recv_sem=irecv_sem.at[k],
            device_id=coords(k), device_id_type=MESH,
        )

    def stats_copy(k):
        return pltpu.make_async_remote_copy(
            src_ref=stats_out, dst_ref=stats_in.at[k],
            send_sem=ssend_sem.at[k], recv_sem=srecv_sem.at[k],
            device_id=coords(k), device_id_type=MESH,
        )

    def each(lo, hi, act):
        def body(k, carry):
            act(k)
            return carry

        lax.fori_loop(lo, hi, body, 0)

    owner = info_ref[0:1, :]
    slot_hi = info_ref[1:2, :].astype(F32)
    slot_lo = info_ref[2:3, :].astype(F32)
    clip = info_ref[3:4, :]

    onehot = (iota((devices, rows), 0) == owner).astype(F32)
    onehot_b = onehot.astype(BF)
    span = 256
    before = (iota((span, span), 0) < iota((span, span), 1)).astype(F32).astype(BF)
    running = jnp.zeros((devices, 1), F32)
    ranks = []
    for start in range(0, rows, span):
        part = onehot[:, start : start + span]
        ahead = dot(onehot_b[:, start : start + span], before) + running
        ranks.append(jnp.sum(part * ahead, axis=0, keepdims=True))
        running = running + jnp.sum(part, axis=1, keepdims=True)
    rank = jnp.concatenate(ranks, axis=1).astype(jnp.int32)
    position = owner * block + rank

    rank_is = (iota((128, rows), 0) == rank).astype(F32).astype(BF)
    contract = (((1,), (1,)), ((), ()))
    ids = 32.0 * lax.dot_general(
        (onehot * slot_hi).astype(BF), rank_is, contract, preferred_element_type=F32
    ) + lax.dot_general((onehot * slot_lo).astype(BF), rank_is, contract, preferred_element_type=F32)
    ids_out[...] = ids[:, None, :]

    feats = feats_ref[...]
    hi = feats.astype(BF)
    mid = (feats - hi.astype(F32)).astype(BF)
    parts = 4
    some = devices // parts
    chunk = some * block
    for p in range(parts):
        pick = (iota((chunk, rows), 0) + p * chunk == position).astype(F32).astype(BF)
        packed[pl.ds(p * chunk, chunk), :] = encode(dot(pick, hi) + dot(pick, mid))
        if p == 0:
            pl.semaphore_wait(barrier, devices - 1)
            each(1, devices, lambda k: ids_copy(k).start())
        each(max(1, p * some), (p + 1) * some, lambda k: row_copy(k).start())
    arrived[0:block, :] = packed[0:block, :]
    ids_in[0] = ids_out[0]

    in_clip = (iota((8, rows), 0) == clip).astype(F32)
    in_clip_b = in_clip.astype(BF)
    counts = jnp.sum(in_clip, axis=1, keepdims=True) * float(width)
    s_hi, s_mid, s_low = split3(feats_ref[...])
    sums = dot(in_clip_b, s_hi) + dot(in_clip_b, s_mid) + dot(in_clip_b, s_low)
    to_groups = group_matrix(channels, width)
    group_sums = dot_exact(sums, to_groups)
    own_lanes = clip_lanes()
    means = jnp.where(iota((8, 128), 1) < GROUPS, group_sums / jnp.maximum(counts, 1.0), 0.0)
    m_hi, m_mid, m_low = split3(dot_exact(means, group_matrix_t(channels, width)))
    by_row = in_clip.T.astype(BF)
    centre = dot(by_row, m_hi) + dot(by_row, m_mid) + dot(by_row, m_low)
    centred = feats_ref[...] - centre
    s_hi, s_mid, s_low = split3(centred * centred)
    squares = dot(in_clip_b, s_hi) + dot(in_clip_b, s_mid) + dot(in_clip_b, s_low)
    group_squares = dot_exact(squares, to_groups)

    def lanes(x):
        return jnp.sum(jnp.where(own_lanes, x, 0.0), axis=0, keepdims=True)

    line = iota((4, 128), 0)
    stats = jnp.where(
        line == 0,
        lanes(group_sums),
        jnp.where(line == 1, lanes(group_squares), lanes(jnp.broadcast_to(counts, (8, 128)))),
    )
    stats_out[...] = stats
    stats_in[0] = stats
    each(1, devices, lambda k: stats_copy(k).start())

    third = rows // 3
    lane = iota((8, 128), 1)
    for p in range(parts):
        lo, end = p * some, (p + 1) * some
        each(max(1, lo), end, lambda k: ids_copy(k).wait_recv())
        pieces = []
        for q in range(chunk // 128):
            piece = jnp.zeros((8, 128), F32)
            for j in range(some):
                shift = j * block - q * 128
                if shift + block <= 0 or shift >= 128:
                    continue
                line8 = jnp.broadcast_to(ids_in[lo + j], (8, 128))
                if shift % 128:
                    line8 = pltpu.roll(line8, shift % 128, 1)
                piece = jnp.where((lane >= shift) & (lane < shift + block), line8, piece)
            pieces.append(piece[0:1])
        targets = jnp.concatenate(pieces, axis=1).astype(jnp.int32)
        each(max(1, lo), end, lambda k: row_copy(k).wait_recv())
        value = decode(arrived[pl.ds(p * chunk, chunk), :])
        v_hi = value.astype(BF)
        v_rest = (value - v_hi.astype(F32)).astype(BF)
        for start in range(0, rows, third):
            at = pl.ds(start, third)
            pick = (iota((third, chunk), 0) + start == targets).astype(F32).astype(BF)
            placed = dot(pick, v_hi) + dot(pick, v_rest)
            if p == 0:
                features_ref[at, :] = placed
            else:
                features_ref[at, :] += placed

    each(1, devices, lambda k: stats_copy(k).wait_recv())
    sums = stats_in[:, 0, :]
    squares = stats_in[:, 1, :]
    counts = stats_in[:, 2, :]
    total = jnp.sum(counts, axis=0, keepdims=True)
    mean = jnp.sum(sums, axis=0, keepdims=True) / total
    off = sums / jnp.maximum(counts, 1.0) - mean
    var = jnp.sum(squares + counts * (off * off), axis=0, keepdims=True) / total
    inv = 1.0 / jnp.sqrt(var + 1e-06)
    spread = group_matrix_t(channels, width)
    clip_mean = dot_exact(jnp.where(own_lanes, mean, 0.0), spread)
    clip_inv = dot_exact(jnp.where(own_lanes, inv, 0.0), spread)
    first_frame = lax.axis_index("frame") * FR_DEV
    plane = HR * WCOL
    first_ref[...] = jnp.zeros_like(first_ref)
    last_ref[...] = jnp.zeros_like(last_ref)
    for t in range(FR_DEV):
        here = iota((8, channels), 0) == clips_ref[first_frame + t]
        mean_t = jnp.sum(jnp.where(here, clip_mean, 0.0), axis=0, keepdims=True)
        inv_t = jnp.sum(jnp.where(here, clip_inv, 0.0), axis=0, keepdims=True)
        normed = (features_ref[pl.ds(t * plane, plane), :] - mean_t) * inv_t
        v = normed * gain_ref[...] + bias_ref[...]
        act = v / (1.0 + jnp.exp(-v))
        for h in range(HR):
            slab = act[h * WCOL : (h + 1) * WCOL].astype(BF)
            act_ref[t, h] = slab
            rounded = slab.astype(F32)
            first_ref[h, t : t + 1, :] = rounded[0:1]
            last_ref[h, t : t + 1, :] = rounded[WCOL - 1 : WCOL]
            if t >= FR_DEV - 2:
                u = t - (FR_DEV - 2)
                firstp_ref[u, h : h + 1, :] = rounded[0:1]
                lastp_ref[u, h : h + 1, :] = rounded[WCOL - 1 : WCOL]

    def sent(k):
        row_copy(k).wait_send()
        ids_copy(k).wait_send()
        stats_copy(k).wait_send()

    each(1, devices, sent)


def decode_kernel(sizes, clips_ref, act_ref, first_ref, last_ref, firstp_ref, lastp_ref, features_ref, bias_ref,
                  w_ref, out_ref, xs, acc, weights, prev, edge, col, corner, colp, cornerp,
                  w_sem, send_sem, recv_sem):
    n_src, n_frame, n_tile = sizes
    s, f, t = lax.axis_index("src"), lax.axis_index("frame"), lax.axis_index("tile")
    channels = act_ref.shape[-1]
    plane = HR * WCOL

    def weight_copy(i):
        return pltpu.make_async_copy(w_ref.at[i], weights.at[i], w_sem.at[i])

    taps_order = [1, 4, 7, 0, 3, 6, 2, 5, 8]
    for i in taps_order:
        weight_copy(i).start()
    for ref in (prev, edge, col, corner, colp, cornerp):
        ref[...] = jnp.zeros_like(ref)

    moves = [(ds, 0, 0) for ds in (-1, 1)]
    moves += [(0, 1, 0)]
    moves += [(ds, 0, dt) for dt in (-1, 1) for ds in (0, -1, 1)]
    moves += [(ds, 1, dt) for dt in (0, -1, 1) for ds in (0, -1, 1)][1:]

    def inside(ds, df, dt):
        return ((s + ds >= 0) & (s + ds < n_src) & (f + df >= 0) & (f + df < n_frame)
                & (t + dt >= 0) & (t + dt < n_tile))

    barrier = pltpu.get_barrier_semaphore()
    heard = jnp.int32(0)
    for ds, df, dt in moves:
        @pl.when(inside(-ds, -df, -dt))
        def _():
            pl.semaphore_signal(barrier, inc=1, device_id=(s - ds, f - df, t - dt), device_id_type=MESH)

        heard = heard + inside(ds, df, dt).astype(jnp.int32)

    for u in range(FR_DEV):
        at = pl.ds(u * plane, plane)
        acc[at, :] = features_ref[at, :] + bias_ref[...]
    pl.semaphore_wait(barrier, heard)

    def copy(i, move):
        ds, df, dt = move
        row = HR - 1 if dt == 1 else 0
        end = 0 if dt == 1 else 1
        side = 0 if ds == 1 else 1
        if ds == 0 and df == 0:
            src, dst = act_ref.at[:, row], edge.at[end]
        elif ds == 0:
            src = act_ref.at[pl.ds(FR_DEV - 2, 2), pl.ds(0, HR)] if dt == 0 else act_ref.at[pl.ds(FR_DEV - 2, 2), row]
            dst = prev.at[:, pl.ds(1, HR)] if dt == 0 else prev.at[:, (HR + 1) * end]
        elif df == 0:
            ref = last_ref if ds == 1 else first_ref
            src, dst = (ref, col.at[side]) if dt == 0 else (ref.at[row], corner.at[side, end])
        else:
            if dt == 0:
                src, dst = lastp_ref if ds == 1 else firstp_ref, colp.at[side]
            else:
                src, dst = (last_ref if ds == 1 else first_ref).at[row], cornerp.at[side, end]
        return pltpu.make_async_remote_copy(
            src_ref=src, dst_ref=dst, send_sem=send_sem.at[i], recv_sem=recv_sem.at[i],
            device_id=(s + ds, f + df, t + dt), device_id_type=MESH,
        )

    for i, move in enumerate(moves):
        @pl.when(inside(*move))
        def _(i=i, move=move):
            copy(i, move).start()

    def arrive(lo, hi):
        for i, move in list(enumerate(moves))[lo:hi]:
            @pl.when(inside(-move[0], -move[1], -move[2]))
            def _(i=i, move=move):
                copy(i, move).wait_recv()

    first_frame = f * FR_DEV

    def add(part, a, lo):
        for j in range(part.shape[0] // plane):
            here = part[j * plane : (j + 1) * plane]
            at = pl.ds((lo + j) * plane, plane)
            if a < 2:
                frame = first_frame + lo + j
                source = frame - 2 + a
                same = (source >= 0) & (clips_ref[jnp.maximum(source, 0)] == clips_ref[frame])
                here = jnp.where(same, here, 0.0)
            acc[at, :] += here

    groups = [(2, 0, 3), (2, 3, 3), (1, 1, 3), (1, 4, 2), (0, 2, 2), (0, 4, 2)]
    mid_lanes = slice(channels, 2 * channels)
    for a, lo, n in groups:
        if lo in (0, 1, 2):
            weight_copy(3 * a + 1).wait()
        u = lo - 2 + a
        lhs = act_ref[u : u + n].reshape(n * plane, channels)
        add(dot(lhs, weights[3 * a + 1, mid_lanes]), a, lo)

    rows32 = iota((WCOL, channels), 0)

    def widen(u, h, here, left, right):
        wide = here.astype(F32)
        xs[u, h, :, 0:channels] = jnp.where(rows32 == 0, left, pltpu.roll(wide, 1, 0)).astype(BF)
        xs[u, h, :, channels : 2 * channels] = here
        xs[u, h, :, 2 * channels :] = jnp.where(
            rows32 == WCOL - 1, right, pltpu.roll(wide, WCOL - 1, 0)
        ).astype(BF)

    arrive(0, 2)

    def widen_own(h, carry):
        for u in range(FR_DEV):
            widen(u + 2, h + 1, act_ref[u, h], col[0, h, u : u + 1], col[1, h, u : u + 1])
        return carry

    lax.fori_loop(0, HR, widen_own, 0)

    def taken(u, n, b, lanes):
        return xs[u : u + n, b : b + HR, :, lanes].reshape(n * plane, -1)

    for a, lo, n in groups:
        u = lo + a
        w = weights.at[3 * a + 1]
        part = dot(taken(u, n, 1, slice(0, channels)), w[0:channels])
        part = part + dot(taken(u, n, 1, slice(2 * channels, 3 * channels)), w[2 * channels : 3 * channels])
        add(part, a, lo)

    arrive(3, 9)
    for end, h in ((0, 0), (1, HR + 1)):
        for u in range(FR_DEV):
            widen(u + 2, h, edge[end, u], corner[0, end, u : u + 1], corner[1, end, u : u + 1])
    for i in (0, 3, 6, 2, 5, 8):
        weight_copy(i).wait()
    every = slice(0, 3 * channels)
    for a, lo, n in groups:
        u = lo + a
        part = dot(taken(u, n, 0, every), weights[3 * a]) + dot(taken(u, n, 2, every), weights[3 * a + 2])
        add(part, a, lo)

    arrive(2, 3)
    arrive(9, len(moves))
    for u in range(2):
        line = FR_DEV - 2 + u
        for h in range(HR + 2):
            if 0 < h < HR + 1:
                left, right = colp[0, u, h - 1 : h], colp[1, u, h - 1 : h]
            else:
                end = h // (HR + 1)
                left, right = cornerp[0, end, line : line + 1], cornerp[1, end, line : line + 1]
            widen(u, h, prev[u, h], left, right)
    for a, n in ((0, 2), (1, 1)):
        part = dot(taken(a, n, 0, every), weights[3 * a])
        part = part + dot(taken(a, n, 1, every), weights[3 * a + 1])
        part = part + dot(taken(a, n, 2, every), weights[3 * a + 2])
        add(part, a, 0)
    for u in range(FR_DEV):
        out_ref[u] = acc[pl.ds(u * plane, plane), :].astype(BF).reshape(HR, WCOL, channels)
    for i, move in enumerate(moves):
        @pl.when(inside(*move))
        def _(i=i, move=move):
            copy(i, move).wait_send()


def shards(feats, row_map, clip_ids, norm_gain, norm_bias, conv_weight, conv_bias):
    rows, channels = feats.shape
    sizes = tuple(lax.axis_size(name) for name in ("src", "frame", "tile"))
    n_src, n_frame, n_tile = sizes
    devices = n_src * n_frame * n_tile
    block = (rows // devices + 15) // 16 * 16
    me = (lax.axis_index("src") * n_frame + lax.axis_index("frame")) * n_tile + lax.axis_index("tile")
    owner = row_map // rows
    slot = row_map % rows
    frame = owner // n_tile % n_frame * FR_DEV + slot // (HR * WCOL)
    frames = jnp.arange(clip_ids.shape[0], dtype=jnp.int32)
    clip = jnp.sum(jnp.where(frames[:, None] == frame[None, :], clip_ids[:, None], 0), axis=0)
    info = jnp.stack([(owner - me) % devices, slot // 32, slot % 32, clip])
    vmem = pl.BlockSpec(memory_space=pltpu.VMEM)
    smem = pl.BlockSpec(memory_space=pltpu.SMEM)
    dma = pltpu.SemaphoreType.DMA
    edge = jax.ShapeDtypeStruct((HR, 8, channels), F32)
    edge_p = jax.ShapeDtypeStruct((2, HR, channels), F32)
    total = devices * block
    features, act, first, last, firstp, lastp = pl.pallas_call(
        functools.partial(reshard_kernel, sizes, block),
        out_shape=(
            jax.ShapeDtypeStruct((rows, channels), F32),
            jax.ShapeDtypeStruct((FR_DEV, HR, WCOL, channels), BF),
            edge,
            edge,
            edge_p,
            edge_p,
        ),
        in_specs=[smem] + [vmem] * 4,
        out_specs=(vmem,) * 6,
        scratch_shapes=[
            pltpu.VMEM((total, channels), CODE),
            pltpu.VMEM((total, channels), CODE),
            pltpu.VMEM((devices, 1, 128), F32),
            pltpu.VMEM((devices, 1, 128), F32),
            pltpu.VMEM((4, 128), F32),
            pltpu.VMEM((devices, 4, 128), F32),
        ] + [dma((devices,))] * 6,
        compiler_params=pltpu.CompilerParams(
            collective_id=0, has_side_effects=True, vmem_limit_bytes=VMEM_LIMIT
        ),
        name="reshard",
    )(clip_ids, info, feats, norm_gain[None], norm_bias[None])
    return pl.pallas_call(
        functools.partial(decode_kernel, sizes),
        out_shape=jax.ShapeDtypeStruct((FR_DEV, HR, WCOL, channels), BF),
        in_specs=[smem] + [vmem] * 7 + [pl.BlockSpec(memory_space=pl.ANY)],
        out_specs=vmem,
        scratch_shapes=[
            pltpu.VMEM((FR_DEV + 2, HR + 2, WCOL, 3 * channels), BF),
            pltpu.VMEM((rows, channels), F32),
            pltpu.VMEM((9, 3 * channels, channels), BF),
            pltpu.VMEM((2, HR + 2, WCOL, channels), BF),
            pltpu.VMEM((2, FR_DEV, WCOL, channels), BF),
            pltpu.VMEM((2, HR, 8, channels), F32),
            pltpu.VMEM((2, 2, 8, channels), F32),
            pltpu.VMEM((2, 2, HR, channels), F32),
            pltpu.VMEM((2, 2, 8, channels), F32),
            dma((9,)),
            dma((17,)),
            dma((17,)),
        ],
        compiler_params=pltpu.CompilerParams(
            collective_id=1, has_side_effects=True, vmem_limit_bytes=VMEM_LIMIT
        ),
        name="halo_conv",
    )(clip_ids, act, first, last, firstp, lastp, features, conv_bias[None],
      conv_weight.reshape(9, 3 * channels, channels))


def solution(mesh):
    placed = (
        P(("src", "frame", "tile"), None),
        P(("src", "frame", "tile")),
        P(),
        P(),
        P(),
        P(),
        P(),
    )
    return jax.shard_map(
        shards,
        mesh=mesh,
        in_specs=placed,
        out_specs=P("frame", "tile", "src", None),
        check_vma=False,
    )
```
